128 devices in a mesh: row: 16 (over z, x), col: 8 (over y, core).
Axes of the slice: x: 4, y: 4, z: 4, core: 2. Of those that a mesh axis runs over, the one named last changes fastest.
Arguments:
- features: bfloat16 [262144, 512], P(('row', 'col')), may hold values from -12 to 12
- targets: bfloat16 [262144, 128], P(('row', 'col')), may hold values from -6 to 6
- primary: float32 [262144, 128], P(('row', 'col')), may hold values from -1.5 to 1.5
- auxiliary: float32 [262144, 128], P(('row', 'col')), may hold values from -1.5 to 1.5
- factors: bfloat16 [2, 2048, 512], replicated, may hold values from -0.125 to 0.125
- spectrum: float32 [2, 512], replicated, may hold values from 1 to 100
- indices: int32 [2, 2048], replicated, may hold values from 0 to 262143, as said below
Outputs:
- primary_out: float32 [262144, 128], P(('row', 'col'))
- auxiliary_out: float32 [262144, 128], P(('row', 'col'))
The draws below stay inside these ranges and needn't reach their ends.
Inputs may be any that keep to these rules, and one draw needn't show every extreme that they name: For each step the 2048 indices are distinct, and entries k * 16 to (k + 1) * 16 - 1 lie among rows k * 2048 to (k + 1) * 2048 - 1, in no particular order; rows k * 2048 and (k + 1) * 2048 - 1 are always among them.
All inputs are finite; a program needn't handle non-finite values.
Results may differ from the reference program's by a relative error of at most 0.0033.
Values may be sent and summed in bfloat16 or wider, within the bound.
No kernel may reach another device: no remote copies, remote signals or barrier semaphores. Data moves between devices by JAX's collectives and lax.ppermute only.
A program may use at most 64 MiB of HBM per device.

```python
import math
import jax
import jax.numpy as jnp
from jax import lax

D = 512
OUT = 128
RANK = 512
BLOCK = 2048
STEPS = 2
ROWS_DEV = 2048
B_DEV = 16
NROWS = 262144


latent_count = 16


latent_scale = 1.4142136


noise_scale = 1.4142136


def draw_indices(key, part):
    key = jax.random.fold_in(key, 7)
    devices = BLOCK // B_DEV
    subkeys = jax.random.split(key, STEPS * devices)

    def pick(subkey):
        first_key, second_key = jax.random.split(subkey)
        middle = jax.random.permutation(first_key, ROWS_DEV - 2)[:B_DEV - 2].astype(jnp.int32) + 1
        ends = jnp.array([0, ROWS_DEV - 1], dtype=jnp.int32)
        chosen_rows = jnp.concatenate([ends, middle])
        order = jax.random.permutation(second_key, B_DEV)
        return chosen_rows[order]
    chosen = jax.vmap(pick)(subkeys).reshape(STEPS, devices, B_DEV)
    offsets = (jnp.arange(devices, dtype=jnp.int32) * ROWS_DEV)[None, :, None]
    return (chosen.astype(jnp.int32) + offsets).reshape(STEPS, BLOCK).astype(jnp.int32)


def draw_features(key, part):
    key = jax.random.fold_in(key, 11)
    mix_key, latent_key, noise_key = jax.random.split(key, 3)
    mixing = jax.random.normal(mix_key, (latent_count, D), jnp.float32) * latent_count ** (-0.5)
    latent = jax.random.normal(latent_key, (NROWS, latent_count), jnp.float32)
    noise = jax.random.normal(noise_key, (NROWS, D), jnp.float32)
    mixed = jnp.zeros((NROWS, D), jnp.float32)
    for level in range(latent_count):
        mixed = mixed + latent[:, level:level + 1] * mixing[level][None, :]
    values = latent_scale * mixed + noise_scale * noise
    return jnp.clip(values, -12.0, 12.0).astype(jnp.bfloat16)


def shard_levels(key, shape, shards, low, high):
    loudness = 1.0
    for axis_at, blocks in shards:
        draws = jax.random.uniform(jax.random.fold_in(jax.random.fold_in(key, 6), axis_at), (blocks,), jnp.float32, low / len(shards), high / len(shards))
        loudness = loudness * jnp.repeat(jnp.exp(draws), shape[axis_at] // blocks).reshape((-1,) + (1,) * (len(shape) - 1 - axis_at))
    return loudness


def centred(own_key, extent, scale, bound, cuts=(), held_as=jnp.bfloat16):
    values = jax.random.normal(own_key, extent, jnp.float32) * scale
    if len(cuts) > 0:
        values = shard_levels(own_key, extent, cuts, -0.22, 0.18) * values
    return jnp.clip(values, min=-bound, max=bound).astype(held_as)


def setup_inputs(seed: int = 0) -> dict:
    key_list = jax.random.split(jax.random.key(seed), 8)
    features = draw_features(jax.random.fold_in(key_list[7], 71), 0)
    targets = centred(key_list[1], (NROWS, OUT), 1.0, 6.0, ((0, 128),))
    primary = centred(key_list[2], (NROWS, OUT), (48 * NROWS ** -0.5), 1.5, ((0, 128),), jnp.float32)
    auxiliary = centred(key_list[3], (NROWS, OUT), (48 * NROWS ** -0.5), 1.5, ((0, 128),), jnp.float32)
    factors = centred(key_list[4], (STEPS, BLOCK, RANK), BLOCK ** -0.5, 0.125)
    spectrum = jnp.clip(jnp.exp(jax.random.uniform(key_list[5], (STEPS, RANK), jnp.float32, math.log(1.0), math.log(100.0))), 1.0, 100.0)
    indices = draw_indices(jax.random.fold_in(key_list[7], 71), 0)
    return dict(features=features, targets=targets, primary=primary, auxiliary=auxiliary, factors=factors, spectrum=spectrum, indices=indices)


ridge_coef = 0.5
shift_rho = 1.0
step_eta = 0.5
beta_coef = 0.8
gamma_coef = 0.3
alpha_coef = 0.6


def kernel_product(block, span_feat, span_blend):
    block_norms = jnp.sum(jnp.square(block.astype(jnp.float32)), axis=1)
    span_norms = jnp.sum(jnp.square(span_feat.astype(jnp.float32)), axis=1)
    inner = jnp.dot(block, span_feat.T, preferred_element_type=jnp.float32)
    dist = block_norms[:, None] + span_norms[None, :] - 2.0 * inner
    kernel = jnp.exp(-dist / (2.0 * block.shape[1])).astype(jnp.bfloat16)
    return jnp.dot(kernel, span_blend, preferred_element_type=jnp.float32)


def reference(features, targets, primary, auxiliary, factors, spectrum, indices):
    blend = alpha_coef * auxiliary + (1.0 - alpha_coef) * primary
    spans = NROWS // ROWS_DEV
    feat_spans = features.reshape(spans, ROWS_DEV, D)
    for step in range(STEPS):
        sampled = indices[step]
        block = features[sampled]
        blend_bf = blend.astype(jnp.bfloat16).reshape(spans, ROWS_DEV, OUT)

        def accumulate(total, pair):
            return total + kernel_product(block, pair[0], pair[1]), None

        start = jnp.zeros((BLOCK, OUT), jnp.float32)
        kernel_sum, unused = lax.scan(accumulate, start, (feat_spans, blend_bf))
        gradient = kernel_sum + ridge_coef * blend[sampled] - targets[sampled].astype(jnp.float32)
        factor = factors[step].astype(jnp.float32)
        coef = 1.0 / (spectrum[step] + shift_rho) - 1.0 / shift_rho
        projected = jnp.dot(factor.T, gradient, precision=lax.Precision.HIGHEST)
        direction = gradient / shift_rho + jnp.dot(factor, coef[:, None] * projected, precision=lax.Precision.HIGHEST)
        primary = blend.at[sampled].add(-step_eta * direction)
        auxiliary = beta_coef * auxiliary + (1.0 - beta_coef) * blend
        auxiliary = auxiliary.at[sampled].add(-gamma_coef * direction)
        blend = alpha_coef * auxiliary + (1.0 - alpha_coef) * primary
    return primary, auxiliary
```

```python
import functools

import jax
import jax.numpy as jnp
from jax import lax
from jax.experimental import pallas as pl
from jax.experimental.pallas import tpu as pltpu
from jax.sharding import Mesh, PartitionSpec as P

STEPS = 2
CHIPS = 64
OWN = 16
ROWS = 2048
D = 512
OUT = 128
LOG2E = 1.4426950408889634
MIB = 1024 * 1024
ALL = ("row", "y", "core")
SAME_CORE = ("row", "y")
TILE_CHIPS = 16
CHUNK = 512
GROUP = 16

ridge_coef = 0.5
shift_rho = 1.0
step_eta = 0.5
beta_coef = 0.8
gamma_coef = 0.3
alpha_coef = 0.6

MOVE = alpha_coef * gamma_coef + (1.0 - alpha_coef) * step_eta
AUX_MOVE = beta_coef * gamma_coef + (1.0 - beta_coef) * MOVE


def chip_index():
    return lax.axis_index("row") * lax.axis_size("y") + lax.axis_index("y")


def nt(a, b):
    return lax.dot_general(a, b, (((1,), (1,)), ((), ())), preferred_element_type=jnp.float32)


def blends(aux, pri):
    blend0 = alpha_coef * aux + (1.0 - alpha_coef) * pri
    aux1 = beta_coef * aux + (1.0 - beta_coef) * blend0
    blend1 = alpha_coef * aux1 + (1.0 - alpha_coef) * blend0
    return blend0, aux1, blend1


def own_row(idx, step, i):
    position = chip_index() * 2 + lax.axis_index("core")
    return idx[step, position * OWN + i] - position * ROWS


def pick_kernel(idx, feat, send, near, rows_ref, sem, send_sem):
    copies = []
    which = lax.broadcasted_iota(jnp.int32, (STEPS * OWN, 1), 0)
    column = jnp.zeros((STEPS * OWN, 1), jnp.int32)
    for at in range(STEPS * OWN):
        row = own_row(idx, at // OWN, at % OWN)
        inside = lax.bitwise_and(row, GROUP - 1)
        first = pl.multiple_of(row - inside, GROUP)
        copies.append(
            pltpu.make_async_copy(
                feat.at[pl.ds(first, GROUP), :], near.at[pl.ds(at * GROUP, GROUP), :], sem.at[at]
            )
        )
        copies[-1].start()
        column = jnp.where(which == at, at * GROUP + inside, column)
    chosen = lax.broadcasted_iota(jnp.int32, (STEPS * OWN, STEPS * OWN * GROUP), 1) == column
    chosen = chosen.astype(jnp.float32).astype(jnp.bfloat16)
    for copy in copies:
        copy.wait()
    rows = jnp.dot(chosen, near[...], preferred_element_type=jnp.float32)
    rows_ref[...] = rows.astype(jnp.bfloat16)
    copies = [
        pltpu.make_async_copy(rows_ref, send.at[chip], send_sem.at[chip]) for chip in range(CHIPS)
    ]
    for copy in copies:
        copy.start()
    for copy in copies:
        copy.wait()


def pick(indices, features):
    return pl.pallas_call(
        pick_kernel,
        out_shape=jax.ShapeDtypeStruct((CHIPS, STEPS * OWN, D), jnp.bfloat16),
        in_specs=[pl.BlockSpec(memory_space=pltpu.SMEM), pl.BlockSpec(memory_space=pl.ANY)],
        out_specs=pl.BlockSpec(memory_space=pl.ANY),
        scratch_shapes=[
            pltpu.VMEM((STEPS * OWN * GROUP, D), jnp.bfloat16),
            pltpu.VMEM((STEPS * OWN, D), jnp.bfloat16),
            pltpu.SemaphoreType.DMA((STEPS * OWN,)),
            pltpu.SemaphoreType.DMA((CHIPS,)),
        ],
        compiler_params=pltpu.CompilerParams(vmem_limit_bytes=58 * MIB),
        name="pick",
    )(indices, features)


def prepare_kernel(idx, tgt, pri, aux, blend_bf, extra, pri_base, aux_base, rows_base):
    blend0, aux1, blend1 = blends(aux[...], pri[...])
    blend_bf[0] = blend0.astype(jnp.bfloat16)
    blend_bf[1] = blend1.astype(jnp.bfloat16)
    pri_base[...] = blend1
    aux_base[...] = beta_coef * aux1 + (1.0 - beta_coef) * blend1
    which = lax.broadcasted_iota(jnp.int32, (STEPS * OWN, 1), 0)
    column = jnp.zeros((STEPS * OWN, 1), jnp.int32)
    for at in range(STEPS * OWN):
        row = own_row(idx, at // OWN, at % OWN)
        column = jnp.where(which == at, row, column)
        here, aux1, here1 = blends(aux[pl.ds(row, 1), :], pri[pl.ds(row, 1), :])
        extra[pl.ds(at, 1), :] = ridge_coef * (here1 if at >= OWN else here)
        rows_base[0, pl.ds(at, 1), :] = here1
        rows_base[1, pl.ds(at, 1), :] = beta_coef * aux1 + (1.0 - beta_coef) * here1
    chosen = lax.broadcasted_iota(jnp.int32, (STEPS * OWN, ROWS), 1) == column
    chosen = chosen.astype(jnp.float32).astype(jnp.bfloat16)
    extra[...] -= jnp.dot(chosen, tgt[...], preferred_element_type=jnp.float32)


def prepare(indices, targets, primary, auxiliary):
    vmem = pl.BlockSpec(memory_space=pltpu.VMEM)
    return pl.pallas_call(
        prepare_kernel,
        out_shape=(
            jax.ShapeDtypeStruct((STEPS, ROWS, OUT), jnp.bfloat16),
            jax.ShapeDtypeStruct((STEPS * OWN, OUT), jnp.float32),
            jax.ShapeDtypeStruct((ROWS, OUT), jnp.float32),
            jax.ShapeDtypeStruct((ROWS, OUT), jnp.float32),
            jax.ShapeDtypeStruct((2, STEPS * OWN, OUT), jnp.float32),
        ),
        in_specs=[pl.BlockSpec(memory_space=pltpu.SMEM)] + [vmem] * 3,
        out_specs=(vmem,) * 5,
        compiler_params=pltpu.CompilerParams(vmem_limit_bytes=16 * MIB),
        name="prepare",
    )(indices, targets, primary, auxiliary)


SCALE = LOG2E / (2.0 * D)


def row_norms(block):
    wide = block.astype(jnp.float32)
    return jnp.sum(wide * wide, axis=1, keepdims=True) * SCALE


def kernel_values(block, block_norms, feat, feat_norms):
    return jnp.exp2(nt(block, feat) * (2.0 * SCALE) - (block_norms + feat_norms))


def norm_row(feat, scale=SCALE):
    wide = feat.astype(jnp.float32)
    wide = wide * wide
    lanes = wide[:, :128]
    for at in range(128, D, 128):
        lanes += wide[:, at:at + 128]
    return jnp.sum(jnp.transpose(lanes), axis=0, keepdims=True) * scale


def product_kernel(block_ref, feat0, feat1, blend0, blend1, out, feat_ref, norms_ref, sems):
    opening = jnp.logical_and(pl.program_id(0) == 0, pl.program_id(1) == 0)
    parts = [(which, at) for which in range(2) for at in range(0, ROWS, CHUNK)]

    def load(which, at):
        return pltpu.make_async_copy(
            (feat0, feat1)[which].at[pl.ds(at, CHUNK), :],
            feat_ref.at[which, pl.ds(at, CHUNK), :],
            sems.at[which, at // CHUNK],
        )

    @pl.when(opening)
    def _():
        for part in parts:
            load(*part).start()
        for part in parts:
            load(*part).wait()
            which, at = part
            norms_ref[which:which + 1, pl.ds(at, CHUNK)] = norm_row(feat_ref[which, pl.ds(at, CHUNK), :])

    block = block_ref[...].reshape(TILE_CHIPS * OWN, D)
    norms = row_norms(block)
    total = jnp.zeros((TILE_CHIPS * OWN, OUT), jnp.float32)
    for which, at in parts:
        part = pl.ds(at, CHUNK)
        kernel = kernel_values(block, norms, feat_ref[which, part, :], norms_ref[which:which + 1, part])
        total += jnp.dot(
            kernel.astype(jnp.bfloat16), (blend0, blend1)[which][0, part, :],
            preferred_element_type=jnp.float32,
        )
    out[...] = total.reshape(out.shape)


def products(block, features, blend_bf):
    tiles = CHIPS // TILE_CHIPS
    blend_spec = pl.BlockSpec((1, ROWS, OUT), lambda s, i: (s, 0, 0))
    return pl.pallas_call(
        product_kernel,
        grid=(STEPS, tiles),
        out_shape=jax.ShapeDtypeStruct((CHIPS, STEPS, OWN, OUT), jnp.float32),
        in_specs=[pl.BlockSpec((TILE_CHIPS, 1, OWN, D), lambda s, i: (i, s, 0, 0))]
        + [pl.BlockSpec(memory_space=pl.ANY)] * 2
        + [blend_spec] * 2,
        out_specs=pl.BlockSpec((TILE_CHIPS, 1, OWN, OUT), lambda s, i: (i, s, 0, 0)),
        scratch_shapes=[
            pltpu.VMEM((2, ROWS, D), jnp.bfloat16),
            pltpu.VMEM((2, ROWS), jnp.float32),
            pltpu.SemaphoreType.DMA((2, ROWS // CHUNK)),
        ],
        compiler_params=pltpu.CompilerParams(vmem_limit_bytes=56 * MIB),
        cost_estimate=pl.CostEstimate(
            flops=2 * 2048 * 4096 * 640, bytes_accessed=9 * MIB, transcendentals=2048 * 4096
        ),
        name="products",
    )(block, *features, *blend_bf)


def cross_kernel(idx_ref, own1, other1, own0, other0, out, token):
    token[...] = jnp.zeros_like(token)
    half = pl.program_id(0)
    tile = pl.program_id(1)
    size = TILE_CHIPS * OWN
    block = jnp.where(half == 0, own1[...], other1[...]).reshape(size, D)
    norms = row_norms(block)
    for which, feat_ref in enumerate((own0, other0)):
        for at in range(0, CHIPS, TILE_CHIPS):
            feat = feat_ref[at:at + TILE_CHIPS, 0].reshape(size, D)
            kernel = kernel_values(block, norms, feat, norm_row(feat))
            left = idx_ref[pl.ds(half, 1), 1, pl.ds(tile, 1), :].reshape(1, size)
            right = idx_ref[which, 0, at // TILE_CHIPS].reshape(1, size)
            left = jnp.transpose(jnp.broadcast_to(left, (size, size)))
            kernel = kernel.astype(jnp.bfloat16).astype(jnp.float32)
            kernel = kernel + jnp.where(left == right, ridge_coef, 0.0)
            start = which * CHIPS * OWN + at * OWN
            out[0, :, :, start:start + size] = kernel.astype(jnp.bfloat16).reshape(TILE_CHIPS, OWN, size)


def cross(own, other, idx):
    tiles = CHIPS // TILE_CHIPS
    tile_spec = pl.BlockSpec((TILE_CHIPS, 1, OWN, D), lambda h, i: (i, 1, 0, 0))
    whole = pl.BlockSpec((CHIPS, 1, OWN, D), lambda h, i: (0, 0, 0, 0))
    return pl.pallas_call(
        cross_kernel,
        grid=(2, tiles),
        out_shape=(
            jax.ShapeDtypeStruct((2, CHIPS, OWN, ROWS), jnp.bfloat16),
            jax.ShapeDtypeStruct((8, 128), jnp.float32),
        ),
        in_specs=[
            pl.BlockSpec((2, STEPS, tiles, TILE_CHIPS * OWN), lambda h, i: (0, 0, 0, 0)),
            tile_spec, tile_spec, whole, whole,
        ],
        out_specs=(
            pl.BlockSpec((1, TILE_CHIPS, OWN, ROWS), lambda h, i: (h, i, 0, 0)),
            pl.BlockSpec((8, 128), lambda h, i: (0, 0)),
        ),
        compiler_params=pltpu.CompilerParams(vmem_limit_bytes=16 * MIB),
        cost_estimate=pl.CostEstimate(
            flops=2 * 2048 * 2048 * 512, bytes_accessed=12 * MIB, transcendentals=2048 * 2048
        ),
        name="cross",
    )(idx, own, other, own, other)


def collect_kernel(received, extra, after, own_grad, send):
    total = jnp.sum(received[...], axis=0) + extra[...]
    own_grad[...] = total
    send[...] = jnp.broadcast_to(total.astype(jnp.bfloat16)[None], send.shape)


def collect(received, extra, after):
    vmem = pl.BlockSpec(memory_space=pltpu.VMEM)
    return pl.pallas_call(
        collect_kernel,
        out_shape=(
            jax.ShapeDtypeStruct((STEPS * OWN, OUT), jnp.float32),
            jax.ShapeDtypeStruct((CHIPS, STEPS * OWN, OUT), jnp.bfloat16),
        ),
        in_specs=[vmem, vmem, pl.BlockSpec(memory_space=pl.ANY)],
        out_specs=(vmem, vmem),
        compiler_params=pltpu.CompilerParams(vmem_limit_bytes=8 * MIB),
        name="collect",
    )(received, extra, after)


def split(x):
    high = x.astype(jnp.bfloat16)
    return high, (x - high.astype(jnp.float32)).astype(jnp.bfloat16)


def split_nt(x, y):
    high, low = split(x)
    both = nt(jnp.concatenate([high, low], axis=0), y)
    return both[: x.shape[0]] + both[x.shape[0]:]


def finish_kernel(
    idx, grads_own, grads_other, own_grad, factors, spectrum, cross_ref, rows_base, pri_in, aux_in,
    pri_out, aux_out, rows, sems,
):
    chip = chip_index()
    core = lax.axis_index("core")
    count = CHIPS * OWN
    coef = 1.0 / (spectrum[...] + shift_rho) - 1.0 / shift_rho

    def factor(step, half):
        return factors[step, :, lax.bitwise_xor(core, half)].reshape(count, D)

    def gradient(step, half):
        grads = grads_other if half else grads_own
        wide = grads[:, step * OWN:(step + 1) * OWN, :].reshape(count, OUT)
        return jnp.transpose(wide.astype(jnp.float32))

    grad0 = [gradient(0, half) for half in range(2)]
    factor0 = [factor(0, half) for half in range(2)]
    projected = jnp.zeros((OUT, D), jnp.float32)
    for half in range(2):
        projected += jnp.dot(
            grad0[half].astype(jnp.bfloat16), factor0[half], preferred_element_type=jnp.float32
        )
    scaled0 = projected * coef[0:1]
    moves = []
    for half in range(2):
        direction = grad0[half] / shift_rho + split_nt(scaled0, factor0[half])
        moves.append((-MOVE * direction).astype(jnp.bfloat16))
    projected = jnp.zeros((OUT, D), jnp.float32)
    for half in range(2):
        grad1 = gradient(1, half)
        for other in range(2):
            part = cross_ref[half, :, :, other * count:(other + 1) * count].reshape(count, count)
            grad1 += nt(moves[other], part)
        both = jnp.dot(
            jnp.concatenate(split(grad1), axis=0), factor(1, half), preferred_element_type=jnp.float32
        )
        projected += both[:OUT] + both[OUT:]
    scaled1 = projected * coef[1:2]

    own_cross = cross_ref[0, chip]
    own0 = own_grad[0:OWN, :]
    own1 = own_grad[OWN:2 * OWN, :]
    for other in range(2):
        own1 += nt(own_cross[:, other * count:(other + 1) * count], moves[other])

    def own_direction(step, grad, scaled):
        high, low = split(scaled)
        mine = factors[step, chip, core]
        return grad / shift_rho + nt(mine, high) + nt(mine, low)

    direction0 = own_direction(0, own0, scaled0)
    direction1 = own_direction(1, own1, scaled1)

    which = lax.broadcasted_iota(jnp.int32, (OWN, 1), 0)
    lanes = lax.broadcasted_iota(jnp.int32, (1, OWN), 1)
    first = jnp.zeros((1, OWN), jnp.int32)
    second = jnp.zeros((OWN, 1), jnp.int32)
    for i in range(OWN):
        first = jnp.where(lanes == i, own_row(idx, 0, i), first)
        second = jnp.where(which == i, own_row(idx, 1, i), second)
    same = first == second
    shared = jnp.zeros((OWN, OUT), jnp.float32)
    for i in range(OWN):
        shared += jnp.where(same[:, i:i + 1], direction0[i:i + 1, :], 0.0)
    for out, moved0, moved1 in ((0, MOVE, step_eta), (1, AUX_MOVE, gamma_coef)):
        rows[out, 0:OWN, :] = rows_base[out, 0:OWN, :] - moved0 * direction0
        rows[out, OWN:2 * OWN, :] = rows_base[out, OWN:2 * OWN, :] - moved0 * shared - moved1 * direction1
    for step in range(STEPS):
        copies = []
        for out, target in enumerate((pri_out, aux_out)):
            for i in range(OWN):
                at = step * OWN + i
                copies.append(
                    pltpu.make_async_copy(
                        rows.at[out, pl.ds(at, 1), :],
                        target.at[pl.ds(own_row(idx, step, i), 1), :],
                        sems.at[out, i],
                    )
                )
                copies[-1].start()
        for copy in copies:
            copy.wait()


def finish(indices, grads, own_grad, factors, spectrum, cross_values, rows_base, pri_base, aux_base):
    vmem = pl.BlockSpec(memory_space=pltpu.VMEM)
    anywhere = pl.BlockSpec(memory_space=pl.ANY)
    return pl.pallas_call(
        finish_kernel,
        out_shape=(jax.ShapeDtypeStruct((ROWS, OUT), jnp.float32),) * 2,
        in_specs=[pl.BlockSpec(memory_space=pltpu.SMEM)] + [vmem] * 7 + [anywhere] * 2,
        out_specs=(anywhere, anywhere),
        input_output_aliases={8: 0, 9: 1},
        scratch_shapes=[
            pltpu.VMEM((2, STEPS * OWN, OUT), jnp.float32),
            pltpu.SemaphoreType.DMA((2, OWN)),
        ],
        compiler_params=pltpu.CompilerParams(vmem_limit_bytes=16 * MIB),
        name="finish",
    )(indices, *grads, own_grad, factors, spectrum, cross_values, rows_base, pri_base, aux_base)


def on_device(features, targets, primary, auxiliary, factors, spectrum, indices):
    core = lax.axis_index("core")
    swap = lambda x: lax.ppermute(x, "core", [(0, 1), (1, 0)])
    exchange = lambda x: lax.all_to_all(x, SAME_CORE, 0, 0, tiled=True)

    send = pick(indices, features)
    other_features = swap(features)
    blend_bf, extra, pri_base, aux_base, rows_base = prepare(indices, targets, primary, auxiliary)
    other_blend = swap(blend_bf)
    by_core = indices.reshape(STEPS, CHIPS, 2, OWN).astype(jnp.float32)
    tiles = CHIPS // TILE_CHIPS
    halves = [lax.dynamic_index_in_dim(by_core, at, 2, False) for at in (core, 1 - core)]
    idx_halves = jnp.stack(halves).reshape(2, STEPS, tiles, TILE_CHIPS * OWN)

    block = exchange(send).reshape(CHIPS, STEPS, OWN, D)
    other_block = swap(block)
    partial = products(block, (features, other_features), (blend_bf, other_blend))
    received = exchange(partial.reshape(CHIPS, STEPS * OWN, OUT))
    cross_values, token = cross(block, other_block, idx_halves)
    own_grad, tosend = collect(received, extra, token)
    grads = exchange(tosend)
    return finish(
        indices,
        (grads, swap(grads)),
        own_grad,
        factors.reshape(STEPS, CHIPS, 2, OWN, D),
        spectrum,
        cross_values,
        rows_base,
        pri_base,
        aux_base,
    )


def solution(mesh):
    inner = Mesh(mesh.devices.reshape(mesh.shape["row"], mesh.shape["col"] // 2, 2), ALL)
    rows = P(ALL, None)
    return jax.shard_map(
        on_device,
        mesh=inner,
        in_specs=(rows, rows, rows, rows, P(), P(), P()),
        out_specs=(rows, rows),
        check_vma=False,
    )
```

```python
import functools

import jax
import jax.numpy as jnp
from jax import lax
from jax.experimental import pallas as pl
from jax.experimental.pallas import tpu as pltpu
from jax.sharding import Mesh, PartitionSpec as P

STEPS = 2
CHIPS = 64
OWN = 16
ROWS = 2048
D = 512
OUT = 128
LOG2E = 1.4426950408889634
MIB = 1024 * 1024
ALL = ("row", "y", "core")
LINE = 16
Y = 4
CHUNK = 512
GROUP = 16
REPEAT = 8
WIDE = 32

ridge_coef = 0.5
shift_rho = 1.0
step_eta = 0.5
beta_coef = 0.8
gamma_coef = 0.3
alpha_coef = 0.6

MOVE = alpha_coef * gamma_coef + (1.0 - alpha_coef) * step_eta
AUX_MOVE = beta_coef * gamma_coef + (1.0 - beta_coef) * MOVE


def chip_index():
    return lax.axis_index("row") * lax.axis_size("y") + lax.axis_index("y")


def nt(a, b):
    return lax.dot_general(a, b, (((1,), (1,)), ((), ())), preferred_element_type=jnp.float32)


def blends(aux, pri):
    blend0 = alpha_coef * aux + (1.0 - alpha_coef) * pri
    aux1 = beta_coef * aux + (1.0 - beta_coef) * blend0
    blend1 = alpha_coef * aux1 + (1.0 - alpha_coef) * blend0
    return blend0, aux1, blend1


def place():
    return lax.axis_index("y") * LINE + lax.axis_index("row")


def own_row(idx, step, i):
    position = chip_index() * 2 + lax.axis_index("core")
    return idx[step, position * OWN + i] - position * ROWS


def pick_kernel(idx, feat, send, near, rows_ref, sem, send_sem):
    copies = []
    which = lax.broadcasted_iota(jnp.int32, (STEPS * OWN, 1), 0)
    column = jnp.zeros((STEPS * OWN, 1), jnp.int32)
    for at in range(STEPS * OWN):
        row = own_row(idx, at // OWN, at % OWN)
        inside = lax.bitwise_and(row, GROUP - 1)
        first = pl.multiple_of(row - inside, GROUP)
        copies.append(
            pltpu.make_async_copy(
                feat.at[pl.ds(first, GROUP), :], near.at[pl.ds(at * GROUP, GROUP), :], sem.at[at]
            )
        )
        copies[-1].start()
        column = jnp.where(which == at, at * GROUP + inside, column)
    chosen = lax.broadcasted_iota(jnp.int32, (STEPS * OWN, STEPS * OWN * GROUP), 1) == column
    chosen = chosen.astype(jnp.float32).astype(jnp.bfloat16)
    for copy in copies:
        copy.wait()
    rows = jnp.dot(chosen, near[...], preferred_element_type=jnp.float32)
    rows_ref[...] = jnp.broadcast_to(rows.astype(jnp.bfloat16)[None], rows_ref.shape)
    copies = [
        pltpu.make_async_copy(rows_ref, send.at[pl.ds(at * REPEAT, REPEAT)], send_sem.at[at])
        for at in range(LINE // REPEAT)
    ]
    for copy in copies:
        copy.start()
    for copy in copies:
        copy.wait()


def pick(indices, features):
    return pl.pallas_call(
        pick_kernel,
        out_shape=jax.ShapeDtypeStruct((LINE, STEPS * OWN, D), jnp.bfloat16),
        in_specs=[pl.BlockSpec(memory_space=pltpu.SMEM), pl.BlockSpec(memory_space=pltpu.HBM)],
        out_specs=pl.BlockSpec(memory_space=pltpu.HBM),
        scratch_shapes=[
            pltpu.VMEM((STEPS * OWN * GROUP, D), jnp.bfloat16),
            pltpu.VMEM((REPEAT, STEPS * OWN, D), jnp.bfloat16),
            pltpu.SemaphoreType.DMA((STEPS * OWN,)),
            pltpu.SemaphoreType.DMA((LINE // REPEAT,)),
        ],
        compiler_params=pltpu.CompilerParams(vmem_limit_bytes=58 * MIB),
        name="pick",
    )(indices, features)


def prepare_kernel(idx, tgt, pri, aux, blend_bf, extra):
    blend0, _, blend1 = blends(aux[...], pri[...])
    blend_bf[:, :OUT] = blend0.astype(jnp.bfloat16)
    blend_bf[:, OUT:] = blend1.astype(jnp.bfloat16)
    which = lax.broadcasted_iota(jnp.int32, (STEPS * OWN, 1), 0)
    column = jnp.zeros((STEPS * OWN, 1), jnp.int32)
    for at in range(STEPS * OWN):
        row = own_row(idx, at // OWN, at % OWN)
        column = jnp.where(which == at, row, column)
        here, _, here1 = blends(aux[pl.ds(row, 1), :], pri[pl.ds(row, 1), :])
        extra[pl.ds(at, 1), :] = ridge_coef * (here1 if at >= OWN else here)
    chosen = lax.broadcasted_iota(jnp.int32, (STEPS * OWN, ROWS), 1) == column
    chosen = chosen.astype(jnp.float32).astype(jnp.bfloat16)
    extra[...] -= jnp.dot(chosen, tgt[...], preferred_element_type=jnp.float32)


def prepare(indices, targets, primary, auxiliary):
    vmem = pl.BlockSpec(memory_space=pltpu.VMEM)
    return pl.pallas_call(
        prepare_kernel,
        out_shape=(
            pltpu.HBM((ROWS, STEPS * OUT), jnp.bfloat16),
            jax.ShapeDtypeStruct((STEPS * OWN, OUT), jnp.float32),
        ),
        in_specs=[pl.BlockSpec(memory_space=pltpu.SMEM)] + [vmem] * 3,
        out_specs=(vmem,) * 2,
        compiler_params=pltpu.CompilerParams(vmem_limit_bytes=16 * MIB),
        name="prepare",
    )(indices, targets, primary, auxiliary)


SCALE = LOG2E / (2.0 * D)


def row_norms(block):
    wide = block.astype(jnp.float32)
    return jnp.sum(wide * wide, axis=1, keepdims=True) * SCALE


def kernel_values(block, block_norms, feat, feat_norms):
    return jnp.exp2(nt(block, feat) * (2.0 * SCALE) - (block_norms + feat_norms))


def norm_row(feat, scale=SCALE):
    wide = feat.astype(jnp.float32)
    wide = wide * wide
    lanes = wide[:, :128]
    for at in range(128, D, 128):
        lanes += wide[:, at:at + 128]
    return jnp.sum(jnp.transpose(lanes), axis=0, keepdims=True) * scale


def product_kernel(*refs, pieces, sums, others, first):
    blocks, (feat0, feat1, blend0, blend1), rest = refs[:pieces], refs[pieces:pieces + 4], refs[pieces + 4:]
    if not first:
        norms_ref, *rest = rest
    back, rest = rest[:sums], rest[sums:]
    copies = []
    if others:
        sources, (out, whole, sems) = rest[:others], rest[others:]
        y = lax.axis_index("y")
        at = 0
        for source, (delta, first) in zip(sources, ((0, 0), (-1, 0), (1, 0), (2, 0), (2, LINE // 2))):
            target = whole.at[lax.bitwise_and(y + delta, Y - 1), pl.ds(first, source.shape[0])]
            copies.append(pltpu.make_async_copy(source, target, sems.at[at]))
            copies[-1].start()
            at += 1
    elif first:
        out, norms_ref = rest
    else:
        out, = rest
    count = LINE * STEPS * OWN
    block = jnp.concatenate([piece[...].reshape(-1, D) for piece in blocks], axis=0)
    norms = row_norms(block)
    total = jnp.zeros((count, STEPS * OUT), jnp.float32)
    behind = None
    for part in [(which, at) for which in range(2) for at in range(0, ROWS, CHUNK)] + [None]:
        ahead = None
        if part is not None:
            which, at = part
            span = pl.ds(at, CHUNK)
            feat = (feat0, feat1)[which][span, :]
            if first:
                norms_ref[which:which + 1, span] = norm_row(feat)
            kernel = kernel_values(block, norms, feat, norms_ref[which:which + 1, span])
            ahead = (kernel.astype(jnp.bfloat16), (blend0, blend1)[which][span, :])
        if behind is not None:
            total += jnp.dot(*behind, preferred_element_type=jnp.float32)
        behind = ahead
    row = lax.broadcasted_iota(jnp.int32, (count, 1), 0)
    first_step = lax.bitwise_and(row, OWN) == 0
    result = jnp.where(first_step, total[:, :OUT], total[:, OUT:]).reshape(out.shape)
    for part in back:
        result += part[...].astype(jnp.float32)
    out[...] = result.astype(out.dtype)
    for copy in copies:
        copy.wait()


def products(pieces, features, blend_bf, norms=(), sums=(), others=()):
    vmem = pl.BlockSpec(memory_space=pltpu.VMEM)
    far = pl.BlockSpec(memory_space=pltpu.HBM)
    shape = (LINE, STEPS * OWN, OUT)
    out_shape = [jax.ShapeDtypeStruct(shape, jnp.float32) if others else pltpu.HBM(shape, jnp.bfloat16)]
    if not norms:
        out_shape.append(jax.ShapeDtypeStruct((2, ROWS), jnp.float32))
    if others:
        out_shape.append(pltpu.HBM((Y, LINE, STEPS * OWN, D), jnp.bfloat16))
    return pl.pallas_call(
        functools.partial(product_kernel, pieces=len(pieces), sums=len(sums), others=len(others), first=not norms),
        out_shape=tuple(out_shape),
        in_specs=[vmem] * (len(pieces) + 4 + len(norms) + len(sums) + len(others)),
        out_specs=(vmem, far if others else vmem)[: len(out_shape)],
        scratch_shapes=[pltpu.SemaphoreType.DMA((len(others),))] if others else [],
        compiler_params=pltpu.CompilerParams(vmem_limit_bytes=16 * MIB),
        cost_estimate=pl.CostEstimate(
            flops=2 * 512 * 4096 * 768, bytes_accessed=MIB, transcendentals=512 * 4096
        ),
        name="products",
    )(*pieces, *features, *blend_bf, *norms, *sums, *others)


def cross_kernel(
    idx, idx_ref, own0, other0, own1, other1, factors, after, weights, own_rows, factor_ref, norms_ref, sems
):
    half = pl.program_id(0)
    tile = pl.program_id(1)
    opening = jnp.logical_and(half == 0, tile == 0)
    core = lax.axis_index("core")
    size = WIDE * OWN
    ones = (own1, other1)
    parts = [(which, at) for which in range(2) for at in range(0, CHIPS, WIDE)]

    def loads(which):
        return [
            pltpu.make_async_copy(
                factors.at[1, :, y, lax.bitwise_xor(core, which)],
                factor_ref.at[which, pl.ds(y * LINE, LINE)],
                sems.at[which, y],
            )
            for y in range(Y)
        ]

    def tile_of(first_tile):
        if first_tile:
            for load in loads(0) + loads(1):
                load.start()
        block = jnp.where(half == 0, own0[...], other0[...]).reshape(size, D)
        norms = row_norms(block)
        here = idx_ref[pl.ds(half, 1), 0, pl.ds(tile, 1), :].reshape(1, size)
        left = jnp.transpose(jnp.broadcast_to(here, (size, size)))
        total = jnp.zeros((size, D), jnp.float32)
        behind = None
        for at, part in enumerate(parts + [None]):
            ahead = None
            if part is not None:
                which, first = part
                feat = ones[which][first:first + WIDE, 0].reshape(size, D)
                if first_tile:
                    norms_ref[at:at + 1, :] = norm_row(feat)
                kernel = kernel_values(block, norms, feat, norms_ref[at:at + 1, :])
                right = idx_ref[which, 1, first // WIDE].reshape(1, size)
                kernel += jnp.where(left == right, ridge_coef, 0.0)
                ahead = (kernel.astype(jnp.bfloat16), which, first)
            if behind is not None:
                values, which, first = behind
                if first_tile and first == 0:
                    for load in loads(which):
                        load.wait()
                factor = factor_ref[which, first:first + WIDE].reshape(size, D)
                total += jnp.dot(values, factor, preferred_element_type=jnp.float32)
            behind = ahead
        weights[...] = total.astype(jnp.bfloat16)

    pl.when(opening)(lambda: tile_of(True))
    pl.when(jnp.logical_not(opening))(lambda: tile_of(False))

    block = jnp.where(half == 0, own0[...], other0[...]).reshape(size, D)
    here = idx_ref[pl.ds(half, 1), 0, pl.ds(tile, 1), :].reshape(1, size)
    mine = own1[place(), 0]
    which_row = lax.broadcasted_iota(jnp.int32, (OWN, 1), 0)
    column = jnp.zeros((OWN, 1), jnp.int32)
    position = chip_index() * 2 + core
    for i in range(OWN):
        column = jnp.where(which_row == i, idx[1, position * OWN + i], column)
    kernel = kernel_values(mine, row_norms(mine), block, norm_row(block))
    kernel += jnp.where(column.astype(jnp.float32) == here, ridge_coef, 0.0)
    own_rows[...] = kernel.astype(jnp.bfloat16)


def cross(indices, own, other, idx, factors, after):
    tiles = CHIPS // WIDE
    tile_spec = pl.BlockSpec((WIDE, 1, OWN, D), lambda h, i: (i, 0, 0, 0))
    whole = pl.BlockSpec((CHIPS, 1, OWN, D), lambda h, i: (0, 1, 0, 0))
    anywhere = pl.BlockSpec(memory_space=pl.ANY)
    size = WIDE * OWN
    own, factors = [pltpu.with_memory_space_constraint(x, pltpu.HBM) for x in (own, factors)]
    return pl.pallas_call(
        cross_kernel,
        grid=(2, tiles),
        out_shape=(
            pltpu.HBM((ROWS, D), jnp.bfloat16),
            jax.ShapeDtypeStruct((OWN, ROWS), jnp.bfloat16),
        ),
        in_specs=[
            pl.BlockSpec(memory_space=pltpu.SMEM),
            pl.BlockSpec((2, STEPS, tiles, size), lambda h, i: (0, 0, 0, 0)),
            tile_spec, tile_spec, whole, whole, pl.BlockSpec(memory_space=pltpu.HBM), anywhere,
        ],
        out_specs=(
            pl.BlockSpec((size, D), lambda h, i: (h * tiles + i, 0)),
            pl.BlockSpec((OWN, size), lambda h, i: (0, h * tiles + i)),
        ),
        scratch_shapes=[
            pltpu.VMEM((2, CHIPS, OWN, D), jnp.bfloat16),
            pltpu.VMEM((2 * tiles, size), jnp.float32),
            pltpu.SemaphoreType.DMA((2, Y)),
        ],
        compiler_params=pltpu.CompilerParams(vmem_limit_bytes=48 * MIB),
        cost_estimate=pl.CostEstimate(
            flops=2 * 2048 * 2048 * 1024, bytes_accessed=8 * MIB, transcendentals=2048 * 2048
        ),
        name="cross",
    )(indices, idx, own, other, own, other, factors, after)


def collect_kernel(received, extra, own_grad, send):
    total = jnp.sum(received[...], axis=0) + extra[...]
    own_grad[...] = total
    send[...] = jnp.broadcast_to(total.astype(jnp.bfloat16)[None], send.shape)


def collect(received, extra):
    vmem = pl.BlockSpec(memory_space=pltpu.VMEM)
    return pl.pallas_call(
        collect_kernel,
        out_shape=(
            jax.ShapeDtypeStruct((STEPS * OWN, OUT), jnp.float32),
            jax.ShapeDtypeStruct((2 * CHIPS, STEPS * OWN, OUT), jnp.bfloat16),
        ),
        in_specs=[vmem, vmem],
        out_specs=(vmem, vmem),
        compiler_params=pltpu.CompilerParams(vmem_limit_bytes=8 * MIB),
        name="collect",
    )(received, extra)


def split(x):
    high = x.astype(jnp.bfloat16)
    return high, (x - high.astype(jnp.float32)).astype(jnp.bfloat16)


def split_nt(x, y):
    high, low = split(x)
    both = nt(jnp.concatenate([high, low], axis=0), y)
    return both[: x.shape[0]] + both[x.shape[0]:]


def finish_kernel(
    idx, grads, own_grad, own_cross, spectrum, factors, weights, pri, aux,
    pri_out, aux_out, result, factor_ref, weights_ref, sems, load_sems, factor_sems,
):
    chip = place()
    core = lax.axis_index("core")
    count = CHIPS * OWN
    loads = [
        pltpu.make_async_copy(
            factors.at[step, :, y, lax.bitwise_xor(core, half)],
            factor_ref.at[step, half, pl.ds(y * LINE, LINE)],
            factor_sems.at[step, half, y],
        )
        for step in range(STEPS) for half in range(2) for y in range(Y)
    ]
    loads.append(pltpu.make_async_copy(weights, weights_ref, load_sems.at[2]))
    for out, source in enumerate((pri, aux)):
        loads.append(pltpu.make_async_copy(source, result.at[out], load_sems.at[out]))
    for load in loads:
        load.start()
    coef = 1.0 / (spectrum[...] + shift_rho) - 1.0 / shift_rho

    def factor(step, half):
        return factor_ref[step, half].reshape(count, D)

    def gradient(step, half):
        other = lax.bitwise_xor(core, half)
        wide = [
            grads[:, y, other, step * OWN:(step + 1) * OWN, :].reshape(LINE * OWN, OUT) for y in range(Y)
        ]
        return jnp.transpose(jnp.concatenate(wide, axis=0).astype(jnp.float32))

    grad0 = [gradient(0, half) for half in range(2)]
    grad1 = [gradient(1, half) for half in range(2)]

    def project(grad, step):
        total = jnp.zeros((OUT, D), jnp.float32)
        for half in range(2):
            total += jnp.dot(
                grad[half].astype(jnp.bfloat16), factor(step, half), preferred_element_type=jnp.float32
            )
        return total

    for load in loads[:2 * Y]:
        load.wait()
    scaled0 = project(grad0, 0) * coef[0:1]
    moves = []
    for half in range(2):
        direction = grad0[half] / shift_rho + split_nt(scaled0, factor(0, half))
        moves.append((-MOVE * direction).astype(jnp.bfloat16))
    for load in loads[2 * Y:]:
        load.wait()
    projected = project(grad1, 1)
    _, aux1, blend1 = blends(result[1], result[0])
    result[0] = blend1
    result[1] = beta_coef * aux1 + (1.0 - beta_coef) * blend1
    for half in range(2):
        projected += jnp.dot(
            moves[half], weights_ref[half * count:(half + 1) * count, :], preferred_element_type=jnp.float32
        )
    scaled1 = projected * coef[1:2]

    own0 = own_grad[0:OWN, :]
    own1 = own_grad[OWN:2 * OWN, :]
    for half in range(2):
        own1 += nt(own_cross[:, half * count:(half + 1) * count], moves[half])

    def own_direction(step, grad, scaled):
        high, low = split(scaled)
        mine = factor_ref[step, 0, chip]
        return grad / shift_rho + nt(mine, high) + nt(mine, low)

    direction0 = own_direction(0, own0, scaled0)
    direction1 = own_direction(1, own1, scaled1)

    for step, direction, moved in (
        (0, direction0, (MOVE, AUX_MOVE)),
        (1, direction1, (step_eta, gamma_coef)),
    ):
        for i in range(OWN):
            row = pl.ds(own_row(idx, step, i), 1)
            for out in range(2):
                result[out, row, :] -= moved[out] * direction[i:i + 1, :]
    stores = []
    for out, target in enumerate((pri_out, aux_out)):
        for at in range(2):
            part = pl.ds(at * (ROWS // 2), ROWS // 2)
            stores.append(pltpu.make_async_copy(result.at[out, part, :], target.at[part, :], sems.at[out, at]))
            stores[-1].start()
    for store in stores:
        store.wait()


def finish(indices, grads, own_grad, own_cross, spectrum, factors, weights, primary, auxiliary):
    vmem = pl.BlockSpec(memory_space=pltpu.VMEM)
    factors, weights, primary, auxiliary = [
        pltpu.with_memory_space_constraint(x, pltpu.HBM) for x in (factors, weights, primary, auxiliary)
    ]
    far = pl.BlockSpec(memory_space=pltpu.HBM)
    return pl.pallas_call(
        finish_kernel,
        out_shape=(pltpu.HBM((ROWS, OUT), jnp.float32),) * 2,
        in_specs=[pl.BlockSpec(memory_space=pltpu.SMEM)] + [vmem] * 4 + [far] * 4,
        out_specs=(far, far),
        scratch_shapes=[
            pltpu.VMEM((2, ROWS, OUT), jnp.float32),
            pltpu.VMEM((STEPS, 2, CHIPS, OWN, D), jnp.bfloat16),
            pltpu.VMEM((ROWS, D), jnp.bfloat16),
            pltpu.SemaphoreType.DMA((2, 2)),
            pltpu.SemaphoreType.DMA((3,)),
            pltpu.SemaphoreType.DMA((STEPS, 2, Y)),
        ],
        compiler_params=pltpu.CompilerParams(vmem_limit_bytes=32 * MIB),
        name="finish",
    )(indices, grads, own_grad, own_cross, spectrum, factors, weights, primary, auxiliary)


def on_device(features, targets, primary, auxiliary, factors, spectrum, indices):
    core = lax.axis_index("core")
    swap = lambda x: lax.ppermute(x, "core", [(0, 1), (1, 0)])
    exchange = lambda x: lax.all_to_all(x, "row", 0, 0, tiled=True)

    def shift(x, by):
        return lax.ppermute(x, "y", [(y, (y + by) % Y) for y in range(Y)])

    send = pick(indices, features)
    other_features = swap(features)
    send, primary, auxiliary = lax.optimization_barrier((send, primary, auxiliary))
    here = exchange(send)
    blend_bf, extra = prepare(indices, targets, primary, auxiliary)
    blend_bf = (blend_bf, swap(blend_bf))
    features = (features, other_features)
    by_core = indices.reshape(STEPS, LINE, Y, 2, OWN).astype(jnp.float32)
    halves = [lax.dynamic_index_in_dim(by_core, at, 3, False) for at in (core, 1 - core)]
    idx_halves = jnp.stack(halves).transpose(0, 1, 3, 2, 4).reshape(2, STEPS, CHIPS // WIDE, WIDE * OWN)

    below = shift(here, 1)
    above = shift(here, -1)
    across = (shift(below[: LINE // 2], 1), shift(above[LINE // 2:], -1))
    to_below, norms = products((below,), features, blend_bf)
    norms = (norms,)
    for_below = shift(to_below, -1)
    above_late, _ = lax.optimization_barrier((above, to_below))
    to_above, = products((above_late,), features, blend_bf, norms)
    for_above = shift(to_above, 1)
    across_late, _ = lax.optimization_barrier((across, to_above))
    to_across, = products(across_late, features, blend_bf, norms)
    for_across = shift(to_across, 2)
    here_late, _ = lax.optimization_barrier((here, to_across))
    partial, block = products(
        (here_late,), features, blend_bf, norms, (for_below, for_above), (here, below, above) + across
    )
    partial = partial + for_across.astype(jnp.float32)
    block, partial = lax.optimization_barrier((block, partial))
    block = block.reshape(CHIPS, STEPS, OWN, D)
    other_block = swap(block)
    received = exchange(partial)
    own_grad, tosend = collect(received, extra)
    factors = factors.reshape(STEPS, LINE, Y, 2, OWN, D)
    weights, own_cross = cross(indices, block, other_block, idx_halves, factors, own_grad)
    grads = lax.all_to_all(tosend, ALL, 0, 0, tiled=True).reshape(LINE, Y, 2, STEPS * OWN, OUT)
    return finish(indices, grads, own_grad, own_cross, spectrum, factors, weights, primary, auxiliary)


def solution(mesh):
    inner = Mesh(mesh.devices.reshape(mesh.shape["row"], mesh.shape["col"] // 2, 2), ALL)
    rows = P(ALL, None)
    return jax.shard_map(
        on_device,
        mesh=inner,
        in_specs=(rows, rows, rows, rows, P(), P(), P()),
        out_specs=(rows, rows),
        check_vma=False,
    )
```

```python
import functools

import jax
import jax.numpy as jnp
from jax import lax
from jax.experimental import pallas as pl
from jax.experimental.pallas import tpu as pltpu
from jax.sharding import Mesh, PartitionSpec as P

STEPS = 2
CHIPS = 64
OWN = 16
ROWS = 2048
D = 512
OUT = 128
LOG2E = 1.4426950408889634
MIB = 1024 * 1024
ALL = ("row", "y", "core")
LINE = 16
Y = 4
CHUNK = 512
GROUP = 16
REPEAT = 8
WIDE = 32

ridge_coef = 0.5
shift_rho = 1.0
step_eta = 0.5
beta_coef = 0.8
gamma_coef = 0.3
alpha_coef = 0.6

MOVE = alpha_coef * gamma_coef + (1.0 - alpha_coef) * step_eta
AUX_MOVE = beta_coef * gamma_coef + (1.0 - beta_coef) * MOVE


def chip_index():
    return lax.axis_index("row") * lax.axis_size("y") + lax.axis_index("y")


def nt(a, b):
    return lax.dot_general(a, b, (((1,), (1,)), ((), ())), preferred_element_type=jnp.float32)


def blends(aux, pri):
    blend0 = alpha_coef * aux + (1.0 - alpha_coef) * pri
    aux1 = beta_coef * aux + (1.0 - beta_coef) * blend0
    blend1 = alpha_coef * aux1 + (1.0 - alpha_coef) * blend0
    return blend0, aux1, blend1


def place():
    return lax.axis_index("y") * LINE + lax.axis_index("row")


def own_row(idx, step, i):
    position = chip_index() * 2 + lax.axis_index("core")
    return idx[step, position * OWN + i] - position * ROWS


def pick_kernel(idx, feat, send, near, rows_ref, sem, send_sem):
    copies = []
    which = lax.broadcasted_iota(jnp.int32, (STEPS * OWN, 1), 0)
    column = jnp.zeros((STEPS * OWN, 1), jnp.int32)
    for at in range(STEPS * OWN):
        row = own_row(idx, at // OWN, at % OWN)
        inside = lax.bitwise_and(row, GROUP - 1)
        first = pl.multiple_of(row - inside, GROUP)
        copies.append(
            pltpu.make_async_copy(
                feat.at[pl.ds(first, GROUP), :], near.at[pl.ds(at * GROUP, GROUP), :], sem.at[at]
            )
        )
        copies[-1].start()
        column = jnp.where(which == at, at * GROUP + inside, column)
    chosen = lax.broadcasted_iota(jnp.int32, (STEPS * OWN, STEPS * OWN * GROUP), 1) == column
    chosen = chosen.astype(jnp.float32).astype(jnp.bfloat16)
    for copy in copies:
        copy.wait()
    rows = jnp.dot(chosen, near[...], preferred_element_type=jnp.float32)
    rows_ref[...] = jnp.broadcast_to(rows.astype(jnp.bfloat16)[None], rows_ref.shape)
    copies = [
        pltpu.make_async_copy(rows_ref, send.at[pl.ds(at * REPEAT, REPEAT)], send_sem.at[at])
        for at in range(LINE // REPEAT)
    ]
    for copy in copies:
        copy.start()
    for copy in copies:
        copy.wait()


def pick(indices, features):
    return pl.pallas_call(
        pick_kernel,
        out_shape=jax.ShapeDtypeStruct((LINE, STEPS * OWN, D), jnp.bfloat16),
        in_specs=[pl.BlockSpec(memory_space=pltpu.SMEM), pl.BlockSpec(memory_space=pltpu.HBM)],
        out_specs=pl.BlockSpec(memory_space=pltpu.HBM),
        scratch_shapes=[
            pltpu.VMEM((STEPS * OWN * GROUP, D), jnp.bfloat16),
            pltpu.VMEM((REPEAT, STEPS * OWN, D), jnp.bfloat16),
            pltpu.SemaphoreType.DMA((STEPS * OWN,)),
            pltpu.SemaphoreType.DMA((LINE // REPEAT,)),
        ],
        compiler_params=pltpu.CompilerParams(vmem_limit_bytes=58 * MIB),
        name="pick",
    )(indices, features)


def prepare_kernel(idx, tgt, pri, aux, other_pri, other_aux, blend_bf, other_blend, extra):
    for a, p, out in ((aux, pri, blend_bf), (other_aux, other_pri, other_blend)):
        blend0, _, blend1 = blends(a[...], p[...])
        out[:, :OUT] = blend0.astype(jnp.bfloat16)
        out[:, OUT:] = blend1.astype(jnp.bfloat16)
    which = lax.broadcasted_iota(jnp.int32, (STEPS * OWN, 1), 0)
    column = jnp.zeros((STEPS * OWN, 1), jnp.int32)
    for at in range(STEPS * OWN):
        row = own_row(idx, at // OWN, at % OWN)
        column = jnp.where(which == at, row, column)
        here, _, here1 = blends(aux[pl.ds(row, 1), :], pri[pl.ds(row, 1), :])
        extra[pl.ds(at, 1), :] = ridge_coef * (here1 if at >= OWN else here)
    chosen = lax.broadcasted_iota(jnp.int32, (STEPS * OWN, ROWS), 1) == column
    chosen = chosen.astype(jnp.float32).astype(jnp.bfloat16)
    extra[...] -= jnp.dot(chosen, tgt[...], preferred_element_type=jnp.float32)


def prepare(indices, targets, *weights):
    vmem = pl.BlockSpec(memory_space=pltpu.VMEM)
    return pl.pallas_call(
        prepare_kernel,
        out_shape=(
            jax.ShapeDtypeStruct((ROWS, STEPS * OUT), jnp.bfloat16),
            jax.ShapeDtypeStruct((ROWS, STEPS * OUT), jnp.bfloat16),
            jax.ShapeDtypeStruct((STEPS * OWN, OUT), jnp.float32),
        ),
        in_specs=[pl.BlockSpec(memory_space=pltpu.SMEM)] + [vmem] * 5,
        out_specs=(vmem,) * 3,
        compiler_params=pltpu.CompilerParams(vmem_limit_bytes=16 * MIB),
        name="prepare",
    )(indices, targets, *weights)


SCALE = LOG2E / (2.0 * D)


def row_norms(block):
    wide = block.astype(jnp.float32)
    return jnp.sum(wide * wide, axis=1, keepdims=True) * SCALE


def kernel_values(block, block_norms, feat, feat_norms):
    return jnp.exp2(nt(block, feat) * (2.0 * SCALE) - (block_norms + feat_norms))


def norm_row(feat, scale=SCALE):
    wide = feat.astype(jnp.float32)
    wide = wide * wide
    lanes = wide[:, :128]
    for at in range(128, D, 128):
        lanes += wide[:, at:at + 128]
    return jnp.sum(jnp.transpose(lanes), axis=0, keepdims=True) * scale


def product_kernel(*refs, pieces, sums, others, first):
    blocks, (feat0, feat1, blend0, blend1), rest = refs[:pieces], refs[pieces:pieces + 4], refs[pieces + 4:]
    if not first:
        norms_ref, *rest = rest
    back, rest = rest[:sums], rest[sums:]
    copies = []
    if others:
        sources, (out, whole, sems) = rest[:others], rest[others:]
        y = lax.axis_index("y")
        at = 0
        for source, (delta, first) in zip(sources, ((0, 0), (-1, 0), (1, 0), (2, 0), (2, LINE // 2))):
            target = whole.at[lax.bitwise_and(y + delta, Y - 1), pl.ds(first, source.shape[0])]
            copies.append(pltpu.make_async_copy(source, target, sems.at[at]))
            copies[-1].start()
            at += 1
    elif first:
        out, norms_ref = rest
    else:
        out, = rest
    count = LINE * STEPS * OWN
    block = jnp.concatenate([piece[...].reshape(-1, D) for piece in blocks], axis=0)
    norms = row_norms(block)
    total = jnp.zeros((count, STEPS * OUT), jnp.float32)
    behind = None
    for part in [(which, at) for which in range(2) for at in range(0, ROWS, CHUNK)] + [None]:
        ahead = None
        if part is not None:
            which, at = part
            span = pl.ds(at, CHUNK)
            feat = (feat0, feat1)[which][span, :]
            if first:
                norms_ref[which:which + 1, span] = norm_row(feat)
            kernel = kernel_values(block, norms, feat, norms_ref[which:which + 1, span])
            ahead = (kernel.astype(jnp.bfloat16), (blend0, blend1)[which][span, :])
        if behind is not None:
            total += jnp.dot(*behind, preferred_element_type=jnp.float32)
        behind = ahead
    row = lax.broadcasted_iota(jnp.int32, (count, 1), 0)
    first_step = lax.bitwise_and(row, OWN) == 0
    result = jnp.where(first_step, total[:, :OUT], total[:, OUT:]).reshape(out.shape)
    for part in back:
        result += part[...].astype(jnp.float32)
    out[...] = result.astype(out.dtype)
    for copy in copies:
        copy.wait()


def products(pieces, features, blend_bf, norms=(), sums=(), others=()):
    vmem = pl.BlockSpec(memory_space=pltpu.VMEM)
    far = pl.BlockSpec(memory_space=pltpu.HBM)
    shape = (LINE, STEPS * OWN, OUT)
    out_shape = [jax.ShapeDtypeStruct(shape, jnp.float32) if others else pltpu.HBM(shape, jnp.bfloat16)]
    if not norms:
        out_shape.append(jax.ShapeDtypeStruct((2, ROWS), jnp.float32))
    if others:
        out_shape.append(pltpu.HBM((Y, LINE, STEPS * OWN, D), jnp.bfloat16))
    return pl.pallas_call(
        functools.partial(product_kernel, pieces=len(pieces), sums=len(sums), others=len(others), first=not norms),
        out_shape=tuple(out_shape),
        in_specs=[vmem] * (len(pieces) + 4 + len(norms) + len(sums) + len(others)),
        out_specs=(vmem, far if others else vmem)[: len(out_shape)],
        scratch_shapes=[pltpu.SemaphoreType.DMA((len(others),))] if others else [],
        compiler_params=pltpu.CompilerParams(vmem_limit_bytes=16 * MIB),
        cost_estimate=pl.CostEstimate(
            flops=2 * 512 * 4096 * 768, bytes_accessed=MIB, transcendentals=512 * 4096
        ),
        name="products",
    )(*pieces, *features, *blend_bf, *norms, *sums, *others)


def cross_kernel(
    idx, idx_ref, own0, other0, own1, other1, factors, after, weights, own_rows, factor_ref, norms_ref, sems
):
    half = pl.program_id(0)
    tile = pl.program_id(1)
    opening = jnp.logical_and(half == 0, tile == 0)
    core = lax.axis_index("core")
    size = WIDE * OWN
    ones = (own1, other1)
    parts = [(which, at) for which in range(2) for at in range(0, CHIPS, WIDE)]

    def loads(which):
        return [
            pltpu.make_async_copy(
                factors.at[1, :, y, lax.bitwise_xor(core, which)],
                factor_ref.at[which, pl.ds(y * LINE, LINE)],
                sems.at[which, y],
            )
            for y in range(Y)
        ]

    def tile_of(first_tile):
        if first_tile:
            for load in loads(0) + loads(1):
                load.start()
        block = jnp.where(half == 0, own0[...], other0[...]).reshape(size, D)
        norms = row_norms(block)
        here = idx_ref[pl.ds(half, 1), 0, pl.ds(tile, 1), :].reshape(1, size)
        left = jnp.transpose(jnp.broadcast_to(here, (size, size)))
        total = jnp.zeros((size, D), jnp.float32)
        behind = None
        for at, part in enumerate(parts + [None]):
            ahead = None
            if part is not None:
                which, first = part
                feat = ones[which][first:first + WIDE, 0].reshape(size, D)
                if first_tile:
                    norms_ref[at:at + 1, :] = norm_row(feat)
                kernel = kernel_values(block, norms, feat, norms_ref[at:at + 1, :])
                right = idx_ref[which, 1, first // WIDE].reshape(1, size)
                kernel += jnp.where(left == right, ridge_coef, 0.0)
                ahead = (kernel.astype(jnp.bfloat16), which, first)
            if behind is not None:
                values, which, first = behind
                if first_tile and first == 0:
                    for load in loads(which):
                        load.wait()
                factor = factor_ref[which, first:first + WIDE].reshape(size, D)
                total += jnp.dot(values, factor, preferred_element_type=jnp.float32)
            behind = ahead
        weights[...] = total.astype(jnp.bfloat16)

    pl.when(opening)(lambda: tile_of(True))
    pl.when(jnp.logical_not(opening))(lambda: tile_of(False))

    block = jnp.where(half == 0, own0[...], other0[...]).reshape(size, D)
    here = idx_ref[pl.ds(half, 1), 0, pl.ds(tile, 1), :].reshape(1, size)
    mine = own1[place(), 0]
    which_row = lax.broadcasted_iota(jnp.int32, (OWN, 1), 0)
    column = jnp.zeros((OWN, 1), jnp.int32)
    position = chip_index() * 2 + core
    for i in range(OWN):
        column = jnp.where(which_row == i, idx[1, position * OWN + i], column)
    kernel = kernel_values(mine, row_norms(mine), block, norm_row(block))
    kernel += jnp.where(column.astype(jnp.float32) == here, ridge_coef, 0.0)
    own_rows[...] = kernel.astype(jnp.bfloat16)


def cross(indices, own, other, idx, factors, after):
    tiles = CHIPS // WIDE
    tile_spec = pl.BlockSpec((WIDE, 1, OWN, D), lambda h, i: (i, 0, 0, 0))
    whole = pl.BlockSpec((CHIPS, 1, OWN, D), lambda h, i: (0, 1, 0, 0))
    anywhere = pl.BlockSpec(memory_space=pl.ANY)
    size = WIDE * OWN
    own, factors = [pltpu.with_memory_space_constraint(x, pltpu.HBM) for x in (own, factors)]
    return pl.pallas_call(
        cross_kernel,
        grid=(2, tiles),
        out_shape=(
            pltpu.HBM((ROWS, D), jnp.bfloat16),
            jax.ShapeDtypeStruct((OWN, ROWS), jnp.bfloat16),
        ),
        in_specs=[
            pl.BlockSpec(memory_space=pltpu.SMEM),
            pl.BlockSpec((2, STEPS, tiles, size), lambda h, i: (0, 0, 0, 0)),
            tile_spec, tile_spec, whole, whole, pl.BlockSpec(memory_space=pltpu.HBM), anywhere,
        ],
        out_specs=(
            pl.BlockSpec((size, D), lambda h, i: (h * tiles + i, 0)),
            pl.BlockSpec((OWN, size), lambda h, i: (0, h * tiles + i)),
        ),
        scratch_shapes=[
            pltpu.VMEM((2, CHIPS, OWN, D), jnp.bfloat16),
            pltpu.VMEM((2 * tiles, size), jnp.float32),
            pltpu.SemaphoreType.DMA((2, Y)),
        ],
        compiler_params=pltpu.CompilerParams(vmem_limit_bytes=48 * MIB),
        cost_estimate=pl.CostEstimate(
            flops=2 * 2048 * 2048 * 1024, bytes_accessed=8 * MIB, transcendentals=2048 * 2048
        ),
        name="cross",
    )(indices, idx, own, other, own, other, factors, after)


def collect_kernel(received, extra, own_grad, send):
    total = jnp.sum(received[...].astype(jnp.float32), axis=0) + extra[...]
    own_grad[...] = total
    send[...] = jnp.broadcast_to(total.astype(jnp.bfloat16)[None], send.shape)


def collect(received, extra):
    vmem = pl.BlockSpec(memory_space=pltpu.VMEM)
    return pl.pallas_call(
        collect_kernel,
        out_shape=(
            jax.ShapeDtypeStruct((STEPS * OWN, OUT), jnp.float32),
            jax.ShapeDtypeStruct((2 * CHIPS, STEPS * OWN, OUT), jnp.bfloat16),
        ),
        in_specs=[vmem, vmem],
        out_specs=(vmem, vmem),
        compiler_params=pltpu.CompilerParams(vmem_limit_bytes=8 * MIB),
        name="collect",
    )(received, extra)


def split(x):
    high = x.astype(jnp.bfloat16)
    return high, (x - high.astype(jnp.float32)).astype(jnp.bfloat16)


def split_nt(x, y):
    high, low = split(x)
    both = nt(jnp.concatenate([high, low], axis=0), y)
    return both[: x.shape[0]] + both[x.shape[0]:]


def finish_kernel(
    idx, grads, own_grad, own_cross, spectrum, factors, weights, pri, aux,
    pri_out, aux_out, result, factor_ref, weights_ref, sems, load_sems, factor_sems,
):
    chip = place()
    core = lax.axis_index("core")
    count = CHIPS * OWN
    loads = [
        pltpu.make_async_copy(
            factors.at[step, :, y, lax.bitwise_xor(core, half)],
            factor_ref.at[step, half, pl.ds(y * LINE, LINE)],
            factor_sems.at[step, half, y],
        )
        for step in range(STEPS) for half in range(2) for y in range(Y)
    ]
    loads.append(pltpu.make_async_copy(weights, weights_ref, load_sems.at[2]))
    for out, source in enumerate((pri, aux)):
        loads.append(pltpu.make_async_copy(source, result.at[out], load_sems.at[out]))
    for load in loads:
        load.start()
    coef = 1.0 / (spectrum[...] + shift_rho) - 1.0 / shift_rho

    def factor(step, half):
        return factor_ref[step, half].reshape(count, D)

    def gradient(step, half):
        other = lax.bitwise_xor(core, half)
        wide = [
            grads[:, y, other, step * OWN:(step + 1) * OWN, :].reshape(LINE * OWN, OUT) for y in range(Y)
        ]
        return jnp.transpose(jnp.concatenate(wide, axis=0).astype(jnp.float32))

    grad0 = [gradient(0, half) for half in range(2)]
    grad1 = [gradient(1, half) for half in range(2)]

    def project(grad, step):
        total = jnp.zeros((OUT, D), jnp.float32)
        for half in range(2):
            total += jnp.dot(
                grad[half].astype(jnp.bfloat16), factor(step, half), preferred_element_type=jnp.float32
            )
        return total

    for load in loads[:2 * Y]:
        load.wait()
    scaled0 = project(grad0, 0) * coef[0:1]
    moves = []
    for half in range(2):
        direction = grad0[half] / shift_rho + split_nt(scaled0, factor(0, half))
        moves.append((-MOVE * direction).astype(jnp.bfloat16))
    for load in loads[2 * Y:]:
        load.wait()
    projected = project(grad1, 1)
    _, aux1, blend1 = blends(result[1], result[0])
    result[0] = blend1
    result[1] = beta_coef * aux1 + (1.0 - beta_coef) * blend1
    for half in range(2):
        projected += jnp.dot(
            moves[half], weights_ref[half * count:(half + 1) * count, :], preferred_element_type=jnp.float32
        )
    scaled1 = projected * coef[1:2]

    own0 = own_grad[0:OWN, :]
    own1 = own_grad[OWN:2 * OWN, :]
    for half in range(2):
        own1 += nt(own_cross[:, half * count:(half + 1) * count], moves[half])

    def own_direction(step, grad, scaled):
        high, low = split(scaled)
        mine = factor_ref[step, 0, chip]
        return grad / shift_rho + nt(mine, high) + nt(mine, low)

    direction0 = own_direction(0, own0, scaled0)
    direction1 = own_direction(1, own1, scaled1)

    for step, direction, moved in (
        (0, direction0, (MOVE, AUX_MOVE)),
        (1, direction1, (step_eta, gamma_coef)),
    ):
        for i in range(OWN):
            row = pl.ds(own_row(idx, step, i), 1)
            for out in range(2):
                result[out, row, :] -= moved[out] * direction[i:i + 1, :]
    stores = []
    for out, target in enumerate((pri_out, aux_out)):
        for at in range(2):
            part = pl.ds(at * (ROWS // 2), ROWS // 2)
            stores.append(pltpu.make_async_copy(result.at[out, part, :], target.at[part, :], sems.at[out, at]))
            stores[-1].start()
    for store in stores:
        store.wait()


def finish(indices, grads, own_grad, own_cross, spectrum, factors, weights, primary, auxiliary):
    vmem = pl.BlockSpec(memory_space=pltpu.VMEM)
    factors, weights, primary, auxiliary = [
        pltpu.with_memory_space_constraint(x, pltpu.HBM) for x in (factors, weights, primary, auxiliary)
    ]
    far = pl.BlockSpec(memory_space=pltpu.HBM)
    return pl.pallas_call(
        finish_kernel,
        out_shape=(pltpu.HBM((ROWS, OUT), jnp.float32),) * 2,
        in_specs=[pl.BlockSpec(memory_space=pltpu.SMEM)] + [vmem] * 4 + [far] * 4,
        out_specs=(far, far),
        scratch_shapes=[
            pltpu.VMEM((2, ROWS, OUT), jnp.float32),
            pltpu.VMEM((STEPS, 2, CHIPS, OWN, D), jnp.bfloat16),
            pltpu.VMEM((ROWS, D), jnp.bfloat16),
            pltpu.SemaphoreType.DMA((2, 2)),
            pltpu.SemaphoreType.DMA((3,)),
            pltpu.SemaphoreType.DMA((STEPS, 2, Y)),
        ],
        compiler_params=pltpu.CompilerParams(vmem_limit_bytes=32 * MIB),
        name="finish",
    )(indices, grads, own_grad, own_cross, spectrum, factors, weights, primary, auxiliary)


def on_device(features, targets, primary, auxiliary, factors, spectrum, indices):
    core = lax.axis_index("core")
    swap = lambda x: lax.ppermute(x, "core", [(0, 1), (1, 0)])
    exchange = lambda x: lax.all_to_all(x, "row", 0, 0, tiled=True)

    def shift(x, by):
        return lax.ppermute(x, "y", [(y, (y + by) % Y) for y in range(Y)])

    send, own = lax.optimization_barrier((pick(indices, features), (features, primary, auxiliary)))
    other_features, other_primary, other_auxiliary = [swap(x) for x in own]
    features = (features, other_features)
    by_core = indices.reshape(STEPS, LINE, Y, 2, OWN).astype(jnp.float32)
    halves = [lax.dynamic_index_in_dim(by_core, at, 3, False) for at in (core, 1 - core)]
    idx_halves = jnp.stack(halves).transpose(0, 1, 3, 2, 4).reshape(2, STEPS, CHIPS // WIDE, WIDE * OWN)

    here = exchange(send)
    below = shift(here, 1)
    above = shift(here, -1)
    weights = (primary, auxiliary, other_primary, other_auxiliary)
    _, weights = lax.optimization_barrier((here, weights))
    *blend_bf, extra = prepare(indices, targets, *weights)
    below, above, blend_bf = lax.optimization_barrier((below, above, blend_bf))
    across = (shift(below[: LINE // 2], 1), shift(above[LINE // 2:], -1))
    to_below, norms = products((below,), features, blend_bf)
    norms = (norms,)
    for_below = shift(to_below, -1)
    above_late, _ = lax.optimization_barrier((above, to_below))
    to_above, = products((above_late,), features, blend_bf, norms)
    for_above = shift(to_above, 1)
    across_late, _ = lax.optimization_barrier((across, to_above))
    to_across, = products(across_late, features, blend_bf, norms)
    for_across = shift(to_across, 2)
    here_late, _ = lax.optimization_barrier((here, to_across))
    partial, block = products(
        (here_late,), features, blend_bf, norms, (for_below, for_above), (here, below, above) + across
    )
    partial = (partial + for_across.astype(jnp.float32)).astype(jnp.bfloat16)
    block, partial = lax.optimization_barrier((block, partial))
    block = block.reshape(CHIPS, STEPS, OWN, D)
    other_block = swap(block)
    received = exchange(partial)
    own_grad, tosend = collect(received, extra)
    factors = factors.reshape(STEPS, LINE, Y, 2, OWN, D)
    weights, own_cross = cross(indices, block, other_block, idx_halves, factors, own_grad)
    grads = lax.all_to_all(tosend, ALL, 0, 0, tiled=True).reshape(LINE, Y, 2, STEPS * OWN, OUT)
    return finish(indices, grads, own_grad, own_cross, spectrum, factors, weights, primary, auxiliary)


def solution(mesh):
    inner = Mesh(mesh.devices.reshape(mesh.shape["row"], mesh.shape["col"] // 2, 2), ALL)
    rows = P(ALL, None)
    return jax.shard_map(
        on_device,
        mesh=inner,
        in_specs=(rows, rows, rows, rows, P(), P(), P()),
        out_specs=(rows, rows),
        check_vma=False,
    )
```

```python
import functools

import jax
import jax.numpy as jnp
from jax import lax
from jax.experimental import pallas as pl
from jax.experimental.pallas import tpu as pltpu
from jax.sharding import Mesh, PartitionSpec as P

STEPS = 2
CHIPS = 64
OWN = 16
ROWS = 2048
D = 512
OUT = 128
LOG2E = 1.4426950408889634
MIB = 1024 * 1024
ALL = ("row", "y", "core")
LINE = 16
Y = 4
CHUNK = 512
GROUP = 16
REPEAT = 8
WIDE = 32

ridge_coef = 0.5
shift_rho = 1.0
step_eta = 0.5
beta_coef = 0.8
gamma_coef = 0.3
alpha_coef = 0.6

MOVE = alpha_coef * gamma_coef + (1.0 - alpha_coef) * step_eta
AUX_MOVE = beta_coef * gamma_coef + (1.0 - beta_coef) * MOVE


def chip_index():
    return lax.axis_index("row") * lax.axis_size("y") + lax.axis_index("y")


def nt(a, b):
    return lax.dot_general(a, b, (((1,), (1,)), ((), ())), preferred_element_type=jnp.float32)


def blends(aux, pri):
    blend0 = alpha_coef * aux + (1.0 - alpha_coef) * pri
    aux1 = beta_coef * aux + (1.0 - beta_coef) * blend0
    blend1 = alpha_coef * aux1 + (1.0 - alpha_coef) * blend0
    return blend0, aux1, blend1


def place():
    return lax.axis_index("y") * LINE + lax.axis_index("row")


def own_row(idx, step, i):
    position = chip_index() * 2 + lax.axis_index("core")
    return idx[step, position * OWN + i] - position * ROWS


def pick_kernel(idx, feat, send, near, rows_ref, sem, send_sem):
    copies = []
    which = lax.broadcasted_iota(jnp.int32, (STEPS * OWN, 1), 0)
    column = jnp.zeros((STEPS * OWN, 1), jnp.int32)
    for at in range(STEPS * OWN):
        row = own_row(idx, at // OWN, at % OWN)
        inside = lax.bitwise_and(row, GROUP - 1)
        first = pl.multiple_of(row - inside, GROUP)
        copies.append(
            pltpu.make_async_copy(
                feat.at[pl.ds(first, GROUP), :], near.at[pl.ds(at * GROUP, GROUP), :], sem.at[at]
            )
        )
        copies[-1].start()
        column = jnp.where(which == at, at * GROUP + inside, column)
    chosen = lax.broadcasted_iota(jnp.int32, (STEPS * OWN, STEPS * OWN * GROUP), 1) == column
    chosen = chosen.astype(jnp.float32).astype(jnp.bfloat16)
    for copy in copies:
        copy.wait()
    rows = jnp.dot(chosen, near[...], preferred_element_type=jnp.float32)
    rows_ref[...] = jnp.broadcast_to(rows.astype(jnp.bfloat16)[None], rows_ref.shape)
    copies = [
        pltpu.make_async_copy(rows_ref, send.at[pl.ds(at * REPEAT, REPEAT)], send_sem.at[at])
        for at in range(LINE // REPEAT)
    ]
    for copy in copies:
        copy.start()
    for copy in copies:
        copy.wait()


def pick(indices, features):
    return pl.pallas_call(
        pick_kernel,
        out_shape=jax.ShapeDtypeStruct((LINE, STEPS * OWN, D), jnp.bfloat16),
        in_specs=[pl.BlockSpec(memory_space=pltpu.SMEM), pl.BlockSpec(memory_space=pltpu.HBM)],
        out_specs=pl.BlockSpec(memory_space=pltpu.HBM),
        scratch_shapes=[
            pltpu.VMEM((STEPS * OWN * GROUP, D), jnp.bfloat16),
            pltpu.VMEM((REPEAT, STEPS * OWN, D), jnp.bfloat16),
            pltpu.SemaphoreType.DMA((STEPS * OWN,)),
            pltpu.SemaphoreType.DMA((LINE // REPEAT,)),
        ],
        compiler_params=pltpu.CompilerParams(vmem_limit_bytes=58 * MIB),
        name="pick",
    )(indices, features)


def prepare_kernel(idx, tgt, pri, aux, other_pri, other_aux, blend_bf, other_blend, extra):
    for a, p, out in ((aux, pri, blend_bf), (other_aux, other_pri, other_blend)):
        blend0, _, blend1 = blends(a[...], p[...])
        out[:, :OUT] = blend0.astype(jnp.bfloat16)
        out[:, OUT:] = blend1.astype(jnp.bfloat16)
    which = lax.broadcasted_iota(jnp.int32, (STEPS * OWN, 1), 0)
    column = jnp.zeros((STEPS * OWN, 1), jnp.int32)
    for at in range(STEPS * OWN):
        row = own_row(idx, at // OWN, at % OWN)
        column = jnp.where(which == at, row, column)
        here, _, here1 = blends(aux[pl.ds(row, 1), :], pri[pl.ds(row, 1), :])
        extra[pl.ds(at, 1), :] = ridge_coef * (here1 if at >= OWN else here)
    chosen = lax.broadcasted_iota(jnp.int32, (STEPS * OWN, ROWS), 1) == column
    chosen = chosen.astype(jnp.float32).astype(jnp.bfloat16)
    extra[...] -= jnp.dot(chosen, tgt[...], preferred_element_type=jnp.float32)


def prepare(indices, targets, *weights):
    vmem = pl.BlockSpec(memory_space=pltpu.VMEM)
    return pl.pallas_call(
        prepare_kernel,
        out_shape=(
            jax.ShapeDtypeStruct((ROWS, STEPS * OUT), jnp.bfloat16),
            jax.ShapeDtypeStruct((ROWS, STEPS * OUT), jnp.bfloat16),
            jax.ShapeDtypeStruct((STEPS * OWN, OUT), jnp.float32),
        ),
        in_specs=[pl.BlockSpec(memory_space=pltpu.SMEM)] + [vmem] * 5,
        out_specs=(vmem,) * 3,
        compiler_params=pltpu.CompilerParams(vmem_limit_bytes=16 * MIB),
        name="prepare",
    )(indices, targets, *weights)


SCALE = LOG2E / (2.0 * D)


def row_norms(block):
    wide = block.astype(jnp.float32)
    return jnp.sum(wide * wide, axis=1, keepdims=True) * SCALE


def kernel_values(block, block_norms, feat, feat_norms):
    return jnp.exp2(nt(block, feat) * (2.0 * SCALE) - (block_norms + feat_norms))


def norm_row(feat, scale=SCALE):
    wide = feat.astype(jnp.float32)
    wide = wide * wide
    lanes = wide[:, :128]
    for at in range(128, D, 128):
        lanes += wide[:, at:at + 128]
    return jnp.sum(jnp.transpose(lanes), axis=0, keepdims=True) * scale


def product_kernel(*refs, pieces, sums, others, first):
    blocks, (feat0, feat1, blend0, blend1), rest = refs[:pieces], refs[pieces:pieces + 4], refs[pieces + 4:]
    if not first:
        norms_ref, *rest = rest
    back, rest = rest[:sums], rest[sums:]
    copies = []
    if others:
        sources, (out, whole, sems) = rest[:others], rest[others:]
        y = lax.axis_index("y")
        at = 0
        for source, (delta, first) in zip(sources, ((0, 0), (-1, 0), (1, 0), (2, 0), (2, LINE // 2))):
            target = whole.at[lax.bitwise_and(y + delta, Y - 1), pl.ds(first, source.shape[0])]
            copies.append(pltpu.make_async_copy(source, target, sems.at[at]))
            copies[-1].start()
            at += 1
    elif first:
        out, norms_ref = rest
    else:
        out, = rest
    count = LINE * STEPS * OWN
    block = jnp.concatenate([piece[...].reshape(-1, D) for piece in blocks], axis=0)
    norms = row_norms(block)
    total = jnp.zeros((count, STEPS * OUT), jnp.float32)
    behind = None
    for part in [(which, at) for which in range(2) for at in range(0, ROWS, CHUNK)] + [None]:
        ahead = None
        if part is not None:
            which, at = part
            span = pl.ds(at, CHUNK)
            feat = (feat0, feat1)[which][span, :]
            if first:
                norms_ref[which:which + 1, span] = norm_row(feat)
            kernel = kernel_values(block, norms, feat, norms_ref[which:which + 1, span])
            ahead = (kernel.astype(jnp.bfloat16), (blend0, blend1)[which][span, :])
        if behind is not None:
            total += jnp.dot(*behind, preferred_element_type=jnp.float32)
        behind = ahead
    row = lax.broadcasted_iota(jnp.int32, (count, 1), 0)
    first_step = lax.bitwise_and(row, OWN) == 0
    result = jnp.where(first_step, total[:, :OUT], total[:, OUT:]).reshape(out.shape)
    for part in back:
        result += part[...].astype(jnp.float32)
    out[...] = result.astype(out.dtype)
    for copy in copies:
        copy.wait()


def products(pieces, features, blend_bf, norms=(), sums=(), others=()):
    vmem = pl.BlockSpec(memory_space=pltpu.VMEM)
    far = pl.BlockSpec(memory_space=pltpu.HBM)
    shape = (LINE, STEPS * OWN, OUT)
    out_shape = [jax.ShapeDtypeStruct(shape, jnp.float32) if others else pltpu.HBM(shape, jnp.bfloat16)]
    if not norms:
        out_shape.append(jax.ShapeDtypeStruct((2, ROWS), jnp.float32))
    if others:
        out_shape.append(pltpu.HBM((Y, LINE, STEPS * OWN, D), jnp.bfloat16))
    return pl.pallas_call(
        functools.partial(product_kernel, pieces=len(pieces), sums=len(sums), others=len(others), first=not norms),
        out_shape=tuple(out_shape),
        in_specs=[vmem] * (len(pieces) + 4 + len(norms) + len(sums) + len(others)),
        out_specs=(vmem, far if others else vmem)[: len(out_shape)],
        scratch_shapes=[pltpu.SemaphoreType.DMA((len(others),))] if others else [],
        compiler_params=pltpu.CompilerParams(vmem_limit_bytes=16 * MIB),
        cost_estimate=pl.CostEstimate(
            flops=2 * 512 * 4096 * 768, bytes_accessed=MIB, transcendentals=512 * 4096
        ),
        name="products",
    )(*pieces, *features, *blend_bf, *norms, *sums, *others)


def cross_kernel(
    idx, idx_ref, own0, other0, own1, other1, factors, after, weights, own_rows, factor_ref, norms_ref, sems
):
    half = pl.program_id(0)
    tile = pl.program_id(1)
    opening = jnp.logical_and(half == 0, tile == 0)
    core = lax.axis_index("core")
    size = WIDE * OWN
    ones = (own1, other1)
    parts = [(which, at) for which in range(2) for at in range(0, CHIPS, WIDE)]

    def loads(which):
        return [
            pltpu.make_async_copy(
                factors.at[1, :, y, lax.bitwise_xor(core, which)],
                factor_ref.at[which, pl.ds(y * LINE, LINE)],
                sems.at[which, y],
            )
            for y in range(Y)
        ]

    def tile_of(first_tile):
        if first_tile:
            for load in loads(0) + loads(1):
                load.start()
        block = jnp.where(half == 0, own0[...], other0[...]).reshape(size, D)
        norms = row_norms(block)
        here = idx_ref[pl.ds(half, 1), 0, pl.ds(tile, 1), :].reshape(1, size)
        left = jnp.transpose(jnp.broadcast_to(here, (size, size)))
        total = jnp.zeros((size, D), jnp.float32)
        behind = None
        for at, part in enumerate(parts + [None]):
            ahead = None
            if part is not None:
                which, first = part
                feat = ones[which][first:first + WIDE, 0].reshape(size, D)
                if first_tile:
                    norms_ref[at:at + 1, :] = norm_row(feat)
                kernel = kernel_values(block, norms, feat, norms_ref[at:at + 1, :])
                right = idx_ref[which, 1, first // WIDE].reshape(1, size)
                kernel += jnp.where(left == right, ridge_coef, 0.0)
                ahead = (kernel.astype(jnp.bfloat16), which, first)
            if behind is not None:
                values, which, first = behind
                if first_tile and first == 0:
                    for load in loads(which):
                        load.wait()
                factor = factor_ref[which, first:first + WIDE].reshape(size, D)
                total += jnp.dot(values, factor, preferred_element_type=jnp.float32)
            behind = ahead
        weights[...] = total.astype(jnp.bfloat16)
        mine = own1[place(), 0]
        which_row = lax.broadcasted_iota(jnp.int32, (OWN, 1), 0)
        column = jnp.zeros((OWN, 1), jnp.int32)
        position = chip_index() * 2 + core
        for i in range(OWN):
            column = jnp.where(which_row == i, idx[1, position * OWN + i], column)
        kernel = kernel_values(mine, row_norms(mine), block, norm_row(block))
        kernel += jnp.where(column.astype(jnp.float32) == here, ridge_coef, 0.0)
        own_rows[...] = kernel.astype(jnp.bfloat16)

    pl.when(opening)(lambda: tile_of(True))
    pl.when(jnp.logical_not(opening))(lambda: tile_of(False))


def cross(indices, own, other, idx, factors, after):
    tiles = CHIPS // WIDE
    tile_spec = pl.BlockSpec((WIDE, 1, OWN, D), lambda h, i: (i, 0, 0, 0))
    whole = pl.BlockSpec((CHIPS, 1, OWN, D), lambda h, i: (0, 1, 0, 0))
    anywhere = pl.BlockSpec(memory_space=pl.ANY)
    size = WIDE * OWN
    own, factors = [pltpu.with_memory_space_constraint(x, pltpu.HBM) for x in (own, factors)]
    return pl.pallas_call(
        cross_kernel,
        grid=(2, tiles),
        out_shape=(
            pltpu.HBM((ROWS, D), jnp.bfloat16),
            jax.ShapeDtypeStruct((OWN, ROWS), jnp.bfloat16),
        ),
        in_specs=[
            pl.BlockSpec(memory_space=pltpu.SMEM),
            pl.BlockSpec((2, STEPS, tiles, size), lambda h, i: (0, 0, 0, 0)),
            tile_spec, tile_spec, whole, whole, pl.BlockSpec(memory_space=pltpu.HBM), anywhere,
        ],
        out_specs=(
            pl.BlockSpec((size, D), lambda h, i: (h * tiles + i, 0)),
            pl.BlockSpec((OWN, size), lambda h, i: (0, h * tiles + i)),
        ),
        scratch_shapes=[
            pltpu.VMEM((2, CHIPS, OWN, D), jnp.bfloat16),
            pltpu.VMEM((2 * tiles, size), jnp.float32),
            pltpu.SemaphoreType.DMA((2, Y)),
        ],
        compiler_params=pltpu.CompilerParams(vmem_limit_bytes=48 * MIB),
        cost_estimate=pl.CostEstimate(
            flops=2 * 2048 * 2048 * 1024, bytes_accessed=8 * MIB, transcendentals=2048 * 2048
        ),
        name="cross",
    )(indices, idx, own, other, own, other, factors, after)


def collect_kernel(received, extra, own_grad, send):
    total = jnp.sum(received[...].astype(jnp.float32), axis=0) + extra[...]
    own_grad[...] = total
    send[...] = jnp.broadcast_to(total.astype(jnp.bfloat16)[None], send.shape)


def collect(received, extra):
    vmem = pl.BlockSpec(memory_space=pltpu.VMEM)
    return pl.pallas_call(
        collect_kernel,
        out_shape=(
            jax.ShapeDtypeStruct((STEPS * OWN, OUT), jnp.float32),
            jax.ShapeDtypeStruct((CHIPS, STEPS * OWN, OUT), jnp.bfloat16),
        ),
        in_specs=[vmem, vmem],
        out_specs=(vmem, vmem),
        compiler_params=pltpu.CompilerParams(vmem_limit_bytes=8 * MIB),
        name="collect",
    )(received, extra)


def split(x):
    high = x.astype(jnp.bfloat16)
    return high, (x - high.astype(jnp.float32)).astype(jnp.bfloat16)


def split_nt(x, y):
    high, low = split(x)
    both = nt(jnp.concatenate([high, low], axis=0), y)
    return both[: x.shape[0]] + both[x.shape[0]:]


def finish_kernel(
    idx, grads0, grads1, own_grad, own_cross, spectrum, factors, weights, pri, aux,
    pri_out, aux_out, result, factor_ref, weights_ref, sems, load_sems, factor_sems,
):
    chip = place()
    core = lax.axis_index("core")
    count = CHIPS * OWN
    loads = [
        pltpu.make_async_copy(
            factors.at[step, :, y, lax.bitwise_xor(core, half)],
            factor_ref.at[step, half, pl.ds(y * LINE, LINE)],
            factor_sems.at[step, half, y],
        )
        for step in range(STEPS) for half in range(2) for y in range(Y)
    ]
    loads.append(pltpu.make_async_copy(weights, weights_ref, load_sems.at[2]))
    for out, source in enumerate((pri, aux)):
        loads.append(pltpu.make_async_copy(source, result.at[out], load_sems.at[out]))
    for load in loads:
        load.start()
    coef = 1.0 / (spectrum[...] + shift_rho) - 1.0 / shift_rho

    def factor(step, half):
        return factor_ref[step, half].reshape(count, D)

    def gradient(step, half):
        grads = (grads0, grads1)[half]
        wide = [grads[:, y, step * OWN:(step + 1) * OWN, :].reshape(LINE * OWN, OUT) for y in range(Y)]
        return jnp.transpose(jnp.concatenate(wide, axis=0).astype(jnp.float32))

    grad0 = [gradient(0, half) for half in range(2)]
    grad1 = [gradient(1, half) for half in range(2)]

    def project(grad, step):
        total = jnp.zeros((OUT, D), jnp.float32)
        for half in range(2):
            total += jnp.dot(
                grad[half].astype(jnp.bfloat16), factor(step, half), preferred_element_type=jnp.float32
            )
        return total

    for load in loads[:2 * Y]:
        load.wait()
    scaled0 = project(grad0, 0) * coef[0:1]
    moves = []
    for half in range(2):
        direction = grad0[half] / shift_rho + split_nt(scaled0, factor(0, half))
        moves.append((-MOVE * direction).astype(jnp.bfloat16))
    for load in loads[2 * Y:4 * Y]:
        load.wait()
    projected = project(grad1, 1)
    for load in loads[4 * Y:]:
        load.wait()
    _, aux1, blend1 = blends(result[1], result[0])
    result[0] = blend1
    result[1] = beta_coef * aux1 + (1.0 - beta_coef) * blend1
    for half in range(2):
        projected += jnp.dot(
            moves[half], weights_ref[half * count:(half + 1) * count, :], preferred_element_type=jnp.float32
        )
    scaled1 = projected * coef[1:2]

    own0 = own_grad[0:OWN, :]
    own1 = own_grad[OWN:2 * OWN, :]
    for half in range(2):
        own1 += nt(own_cross[:, half * count:(half + 1) * count], moves[half])

    def own_direction(step, grad, scaled):
        high, low = split(scaled)
        mine = factor_ref[step, 0, chip]
        return grad / shift_rho + nt(mine, high) + nt(mine, low)

    direction0 = own_direction(0, own0, scaled0)
    direction1 = own_direction(1, own1, scaled1)

    for step, direction, moved in (
        (0, direction0, (MOVE, AUX_MOVE)),
        (1, direction1, (step_eta, gamma_coef)),
    ):
        for i in range(OWN):
            row = pl.ds(own_row(idx, step, i), 1)
            for out in range(2):
                result[out, row, :] -= moved[out] * direction[i:i + 1, :]
    stores = []
    for out, target in enumerate((pri_out, aux_out)):
        for at in range(2):
            part = pl.ds(at * (ROWS // 2), ROWS // 2)
            stores.append(pltpu.make_async_copy(result.at[out, part, :], target.at[part, :], sems.at[out, at]))
            stores[-1].start()
    for store in stores:
        store.wait()


def finish(indices, grads, own_grad, own_cross, spectrum, factors, weights, primary, auxiliary):
    vmem = pl.BlockSpec(memory_space=pltpu.VMEM)
    factors, weights, primary, auxiliary = [
        pltpu.with_memory_space_constraint(x, pltpu.HBM) for x in (factors, weights, primary, auxiliary)
    ]
    far = pl.BlockSpec(memory_space=pltpu.HBM)
    return pl.pallas_call(
        finish_kernel,
        out_shape=(pltpu.HBM((ROWS, OUT), jnp.float32),) * 2,
        in_specs=[pl.BlockSpec(memory_space=pltpu.SMEM)] + [vmem] * 5 + [far] * 4,
        out_specs=(far, far),
        scratch_shapes=[
            pltpu.VMEM((2, ROWS, OUT), jnp.float32),
            pltpu.VMEM((STEPS, 2, CHIPS, OWN, D), jnp.bfloat16),
            pltpu.VMEM((ROWS, D), jnp.bfloat16),
            pltpu.SemaphoreType.DMA((2, 2)),
            pltpu.SemaphoreType.DMA((3,)),
            pltpu.SemaphoreType.DMA((STEPS, 2, Y)),
        ],
        compiler_params=pltpu.CompilerParams(vmem_limit_bytes=32 * MIB),
        name="finish",
    )(indices, *grads, own_grad, own_cross, spectrum, factors, weights, primary, auxiliary)


def on_device(features, targets, primary, auxiliary, factors, spectrum, indices):
    core = lax.axis_index("core")
    swap = lambda x: lax.ppermute(x, "core", [(0, 1), (1, 0)])
    exchange = lambda x: lax.all_to_all(x, "row", 0, 0, tiled=True)

    def shift(x, by):
        return lax.ppermute(x, "y", [(y, (y + by) % Y) for y in range(Y)])

    send, own = lax.optimization_barrier((pick(indices, features), (features, primary, auxiliary)))
    other_features, other_primary, other_auxiliary = [swap(x) for x in own]
    features = (features, other_features)
    by_core = indices.reshape(STEPS, LINE, Y, 2, OWN).astype(jnp.float32)
    halves = [lax.dynamic_index_in_dim(by_core, at, 3, False) for at in (core, 1 - core)]
    idx_halves = jnp.stack(halves).transpose(0, 1, 3, 2, 4).reshape(2, STEPS, CHIPS // WIDE, WIDE * OWN)

    here = exchange(send)
    below = shift(here, 1)
    above = shift(here, -1)
    weights = (primary, auxiliary, other_primary, other_auxiliary)
    _, weights = lax.optimization_barrier((here, weights))
    *blend_bf, extra = prepare(indices, targets, *weights)
    below, above, blend_bf = lax.optimization_barrier((below, above, blend_bf))
    across = (shift(below[: LINE // 2], 1), shift(above[LINE // 2:], -1))
    to_below, norms = products((below,), features, blend_bf)
    norms = (norms,)
    for_below = shift(to_below, -1)
    above_late, _ = lax.optimization_barrier((above, to_below))
    to_above, = products((above_late,), features, blend_bf, norms)
    for_above = shift(to_above, 1)
    across_late, _ = lax.optimization_barrier((across, to_above))
    to_across, = products(across_late, features, blend_bf, norms)
    for_across = shift(to_across, 2)
    here_late, _ = lax.optimization_barrier((here, to_across))
    partial, block = products(
        (here_late,), features, blend_bf, norms, (for_below, for_above), (here, below, above) + across
    )
    partial = (partial + for_across.astype(jnp.float32)).astype(jnp.bfloat16)
    block, partial = lax.optimization_barrier((block, partial))
    block = block.reshape(CHIPS, STEPS, OWN, D)
    other_block = swap(block)
    received = exchange(partial)
    own_grad, tosend = collect(received, extra)
    factors = factors.reshape(STEPS, LINE, Y, 2, OWN, D)
    weights, own_cross = cross(indices, block, other_block, idx_halves, factors, own_grad)
    grads = lax.all_to_all(tosend, ("row", "y"), 0, 0, tiled=True).reshape(LINE, Y, STEPS * OWN, OUT)
    grads, weights = lax.optimization_barrier((grads, weights))
    grads = (grads, swap(grads))
    return finish(indices, grads, own_grad, own_cross, spectrum, factors, weights, primary, auxiliary)


def solution(mesh):
    inner = Mesh(mesh.devices.reshape(mesh.shape["row"], mesh.shape["col"] // 2, 2), ALL)
    rows = P(ALL, None)
    return jax.shard_map(
        on_device,
        mesh=inner,
        in_specs=(rows, rows, rows, rows, P(), P(), P()),
        out_specs=(rows, rows),
        check_vma=False,
    )
```
